1024 devices in a mesh: replica: 64 (over z_lo, x), mp: 16 (over y, z_hi, core).
Axes of the slice: x: 4, y: 4, z: 32 (z_hi: 2, z_lo: 16; z = z_hi * 16 + z_lo), core: 2. Of those that a mesh axis runs over, the one named last changes fastest.
Arguments:
- local_weights: bfloat16 [64, 256, 28672], P('replica', None, 'mp'), may hold values from -16 to 16
- outer_base: float32 [256, 28672], P(None, 'mp'), may hold values from -6 to 6
- outer_momentum: float32 [256, 28672], P(None, 'mp'), may hold values from -6 to 6
- tokens: bfloat16 [65536, 8192], P('replica', 'mp'), may hold values from -6 to 6
- key_value_weight: bfloat16 [8192, 2048], P('mp'), may hold values from -0.09375 to 0.09375
Outputs:
- updated_base: float32 [256, 28672], P('replica', 'mp')
- updated_momentum: float32 [256, 28672], P('replica', 'mp')
- synced_weights: bfloat16 [256, 28672], P(None, 'mp')
- keys_values: bfloat16 [65536, 2048], P('replica', 'mp')
The draws below stay inside these ranges and needn't reach their ends.
All inputs are finite; a program needn't handle non-finite values.
Results may differ from the reference program's by a relative error of at most 0.017.
Values may be sent and summed in bfloat16 or wider, within the bound.
No kernel may reach another device: no remote copies, remote signals or barrier semaphores. Data moves between devices by JAX's collectives and lax.ppermute only.
A program may use at most 64 MiB of HBM per device.

```python
import jax
import jax.numpy as jnp
from jax import lax

D = 8192
FF = 28672
KVW = 2048
PROWS = 256
REPLICAS = 64
TOKENS = 65536
N_MP = 16


def with_spikes(drawn, stream_key, source, target, blocks, factor):
    owner, partner = [(jnp.arange(drawn.shape[dim]) // (drawn.shape[dim] // blocks)).reshape([-1 if axis == dim else 1 for axis in range(drawn.ndim)]) for dim in (source, target)]
    chosen = jax.random.permutation(stream_key, blocks)[partner]
    strong = (owner == chosen) | (owner == (partner + blocks // 2) % blocks)
    return jnp.where(strong, factor * drawn, drawn)


def steps_of(key, shape, split, low, largest):
    gain, own = 1.0, jax.random.fold_in(key, 6)
    for position, blocks in split:
        draws = jnp.exp(jax.random.uniform(jax.random.fold_in(own, position), (blocks,), jnp.float32, low / len(split), largest / len(split)))
        gain = gain * jnp.repeat(draws, shape[position] // blocks).reshape([-1 if axis == position else 1 for axis in range(len(shape))])
    return gain


def centred(key, shape, deviation, reach, cuts=(), held_as=jnp.bfloat16):
    drawn = jax.random.normal(key, shape, jnp.float32) * deviation
    if len(cuts) > 0:
        drawn = steps_of(key, shape, cuts, -0.22, 0.18) * drawn
    return jnp.clip(drawn, min=-reach, max=reach).astype(held_as)


def noise_with(rng, dims, spread, reach, cuts, heavy, kind=jnp.bfloat16):
    result = spread * jax.random.normal(rng, dims, jnp.float32)
    if cuts:
        result = result * steps_of(rng, dims, cuts, -0.22, 0.18)
    return jnp.clip(with_spikes(result, jax.random.fold_in(rng, 3), *heavy), -reach, reach).astype(kind)


def setup_inputs(seed: int = 0) -> dict:
    key_list = jax.random.split(jax.random.key(seed), 6)
    local_weights = noise_with(key_list[0], (REPLICAS, PROWS, FF), 1.0, 16.0, ((0, 64), (2, 16)), (0, 1, 64, 4.0))
    outer_base = centred(key_list[1], (PROWS, FF), 1.0, 6.0, ((1, 16),), jnp.float32)
    outer_momentum = centred(key_list[2], (PROWS, FF), 1.0, 6.0, ((1, 16),), jnp.float32)
    tokens = centred(key_list[3], (TOKENS, D), 1.0, 6.0, ((0, 64), (1, 16)))
    key_value_weight = noise_with(key_list[4], (D, KVW), D ** -0.5, 0.09375, ((0, 16),), (0, 1, 16, 2.0))
    return {"local_weights": local_weights, "outer_base": outer_base, "outer_momentum": outer_momentum, "tokens": tokens, "key_value_weight": key_value_weight}


def reference(local_weights, outer_base, outer_momentum, tokens, key_value_weight):
    anchor = lax.optimization_barrier(outer_base.astype(jnp.bfloat16)).astype(jnp.float32)

    def add_group(replica_index, running):
        piece = lax.dynamic_index_in_dim(local_weights, replica_index, 0, keepdims=False)
        return running + piece.astype(jnp.float32)

    summed = lax.fori_loop(0, REPLICAS, add_group, jnp.zeros(outer_base.shape, jnp.float32))
    outer_grad = anchor - summed / REPLICAS
    updated_momentum = 0.9 * outer_momentum + outer_grad
    updated_base = outer_base - 0.7 * (outer_grad + 0.9 * updated_momentum)
    synced_weights = updated_base.astype(jnp.bfloat16)
    block_width = D // N_MP
    kv_total = jnp.zeros((tokens.shape[0], key_value_weight.shape[1]), jnp.float32)
    for block in range(N_MP):
        start = block * block_width
        kv_partial = jnp.dot(tokens[:, start:start + block_width], key_value_weight[start:start + block_width], preferred_element_type=jnp.float32).astype(jnp.bfloat16)
        kv_total = kv_total + kv_partial.astype(jnp.float32)
    keys_values = kv_total.astype(jnp.bfloat16)
    return (updated_base, updated_momentum, synced_weights, keys_values)
```

```python
import jax
import jax.numpy as jnp
from jax import lax
from jax.experimental import pallas as pl
from jax.experimental.pallas import tpu as pltpu
from jax.sharding import Mesh, PartitionSpec as P

SIZES = (4, 4, 4, 4, 2, 2)
NAMES = ("zo", "zi", "x", "y", "h", "c")
LANES = 128
CHUNKS = 2

bf16 = jnp.bfloat16
f32 = jnp.float32


def shift(axis, size, step):
    return [(i, (i + step) % size) for i in range(size)]


def column(block, h, c):
    return pl.multiple_of((block * 4 + h * 2 + c) * LANES, LANES)


def pack_kernel(blocks, place_ref, weight_ref, packed_ref):
    h, c = place_ref[0], place_ref[1]
    for block in range(blocks):
        for k, side in enumerate((h, 1 - h)):
            to = (2 * block + k) * LANES
            packed_ref[:, to : to + LANES] = weight_ref[:, pl.ds(column(block, side, 1 - c), LANES)]


def project_kernel(blocks, place_ref, own_ref, sibling_ref, weight_ref, packed_ref, out_ref):
    h, c = place_ref[0], place_ref[1]
    own, sibling = own_ref[...], sibling_ref[...]
    for block in range(blocks):
        mine = jnp.concatenate(
            [weight_ref[:, pl.ds(column(block, side, c), LANES)] for side in (h, 1 - h)], axis=1
        )
        width = 2 * LANES
        total = jnp.dot(own, mine, preferred_element_type=f32)
        total += jnp.dot(
            sibling, packed_ref[:, block * width : (block + 1) * width], preferred_element_type=f32
        )
        out_ref[block] = total.astype(bf16)


def pack(place, weight, blocks):
    depth, width = weight.shape
    return pl.pallas_call(
        lambda *refs: pack_kernel(blocks, *refs),
        out_shape=jax.ShapeDtypeStruct((depth, width // 2), bf16),
        grid_spec=pltpu.PrefetchScalarGridSpec(
            num_scalar_prefetch=1,
            grid=(2,),
            in_specs=[pl.BlockSpec((depth // 2, width), lambda i, _: (i, 0))],
            out_specs=pl.BlockSpec((depth // 2, width // 2), lambda i, _: (i, 0)),
        ),
        cost_estimate=pl.CostEstimate(flops=0, bytes_accessed=weight.size * 3, transcendentals=0),
        compiler_params=pltpu.CompilerParams(vmem_limit_bytes=32 << 20),
    )(place, weight)


def project(place, own, sibling, weight, packed, blocks, chunk, rows):
    depth, width = weight.shape
    tile = min(rows, 256)
    first = chunk * (rows // tile)
    return pl.pallas_call(
        lambda *refs: project_kernel(blocks, *refs),
        out_shape=jax.ShapeDtypeStruct((blocks, rows, 2 * LANES), bf16),
        grid_spec=pltpu.PrefetchScalarGridSpec(
            num_scalar_prefetch=1,
            grid=(rows // tile,),
            in_specs=[
                pl.BlockSpec((tile, depth), lambda i, _: (first + i, 0)),
                pl.BlockSpec((tile, depth), lambda i, _: (first + i, 0)),
                pl.BlockSpec((depth, width), lambda i, _: (0, 0)),
                pl.BlockSpec((depth, width // 2), lambda i, _: (0, 0)),
            ],
            out_specs=pl.BlockSpec((blocks, tile, 2 * LANES), lambda i, _: (0, i, 0)),
        ),
        cost_estimate=pl.CostEstimate(
            flops=2 * rows * depth * width, bytes_accessed=rows * depth * 8 + weight.size * 3, transcendentals=0
        ),
        compiler_params=pltpu.CompilerParams(vmem_limit_bytes=32 << 20),
    )(place, own, sibling, weight, packed)


def after(array, *earlier):
    return lax.optimization_barrier((array, *earlier))[0]


def one_hot(source, count):
    return (source[:, None] == jnp.arange(count, dtype=jnp.int32)[None, :]).astype(bf16)


def select_rows(source, array):
    return jnp.dot(one_hot(source, array.shape[0]), array, preferred_element_type=f32).astype(bf16)


def gather_small(array, axis, size):
    copies = jnp.broadcast_to(array, (size, *array.shape))
    return lax.all_to_all(copies, axis, split_axis=0, concat_axis=0, tiled=True)


def shards(local_weights, base, momentum, tokens, weight):
    sizes = dict(zip(NAMES, SIZES))
    zo, zi, x, h, c = (lax.axis_index(a) for a in ("zo", "zi", "x", "h", "c"))
    n_zo, n_zi, n_x, n_y = (sizes[a] for a in ("zo", "zi", "x", "y"))
    swap = [(0, 1), (1, 0)]
    terms = local_weights[0]

    place = jnp.stack([h, c]).astype(jnp.int32)
    sibling = lax.ppermute(tokens, "c", swap)
    packed = pack(place, weight, n_y)
    terms = after(terms, packed)
    packed = lax.ppermute(packed, "c", swap)

    groups = n_zo * n_zi * n_x
    rows, width = base.shape
    own = rows // groups
    per_x = rows // n_x
    at = jnp.arange(per_x, dtype=jnp.int32)
    in_zi, in_zo, in_own = at // (n_zo * own), (at // own) % n_zo, at % own

    def rows_of(at_x):
        return ((in_zo * n_zi + in_zi) * n_x + at_x) * own + in_own

    received = []
    for step in range(1, n_x):
        sent = select_rows(rows_of((x + step) % n_x), terms)
        received.append(lax.ppermute(sent, "x", shift("x", n_x, step)))

    count = tokens.shape[0] // CHUNKS

    def over_y(chunk, *earlier):
        part = project(place, tokens, sibling, weight, packed, n_y, chunk, count)
        part = after(part, *earlier)
        part = lax.all_to_all(part, "y", split_axis=0, concat_axis=0, tiled=True)
        total = part.astype(f32).sum(axis=0)
        return lax.optimization_barrier((total[:, :LANES], total[:, LANES:].astype(bf16)))

    mine0, other0 = over_y(0)
    other0_there = lax.ppermute(other0, "h", swap)

    anchor = select_rows(rows_of(x), base.astype(bf16)).astype(f32)
    total = select_rows(rows_of(x), terms).astype(f32) - n_x * anchor
    received = [after(piece, other0) for piece in received]
    for piece in received:
        total += piece.astype(f32)
    part = lax.all_to_all(total.astype(bf16), "zi", split_axis=0, concat_axis=0, tiled=True)
    part = part.reshape(n_zi, n_zo * own, width)

    mine1, other1 = over_y(1, part)
    other1_there = lax.ppermute(other1, "h", swap)

    start = ((zo * n_zi + zi) * n_x + x) * own
    r = jnp.arange(rows, dtype=jnp.int32)
    from_x, from_zi, from_zo = (r // own) % n_x, (r // (own * n_x)) % n_zi, r // (own * n_x * n_zi)
    where = (from_zi * n_zo + from_zo) * own + r % own + ((x - from_x) % n_x) * per_x

    def finish(part):
        part = part.reshape(n_zi, n_zo * own, width)
        total = part.astype(f32).sum(axis=0).astype(bf16).reshape(n_zo, own, width)
        part = lax.all_to_all(total, "zo", split_axis=0, concat_axis=0, tiled=True)
        outer_grad = -part.astype(f32).sum(axis=0) / groups
        own_base = lax.dynamic_slice_in_dim(base, start, own, 0)
        own_momentum = lax.dynamic_slice_in_dim(momentum, start, own, 0)
        new_momentum = 0.9 * own_momentum + outer_grad
        new_base = own_base - 0.7 * (outer_grad + 0.9 * new_momentum)
        gathered = gather_small(new_base.astype(bf16), "zo", n_zo).reshape(n_zo * own, width)
        gathered = gather_small(gathered, "zi", n_zi).reshape(per_x, width)
        pieces = [gathered] + [lax.ppermute(gathered, "x", shift("x", n_x, step)) for step in range(1, n_x)]
        return gathered, new_base, new_momentum, select_rows(where, jnp.concatenate(pieces, axis=0))

    once = 1 + (h >> 4)
    part = after(part, other0, other1).reshape(per_x, width)
    empty = (part, jnp.zeros((own, width), f32), jnp.zeros((own, width), f32), jnp.zeros((rows, width), bf16))
    _, new_base, new_momentum, synced = lax.fori_loop(0, once, lambda _, carry: finish(carry[0]), empty)

    results = []
    for mine, there in ((mine0, other0_there), (mine1, other1_there)):
        there = after(there, new_base, synced)
        results.append((mine + there.astype(f32)).astype(bf16))
    keys_values = jnp.concatenate(results, axis=0)
    return new_base, new_momentum, synced, keys_values


def solution(mesh):
    fine = Mesh(mesh.devices.reshape(SIZES), NAMES)
    replica, mp = NAMES[:3], NAMES[3:]
    return jax.shard_map(
        shards,
        mesh=fine,
        in_specs=(
            P(replica, None, mp),
            P(None, mp),
            P(None, mp),
            P(replica, mp),
            P(mp, None),
        ),
        out_specs=(P(replica, mp), P(replica, mp), P(None, mp), P(replica, mp)),
        check_vma=False,
    )
```

```python
import jax
import jax.numpy as jnp
from jax import lax
from jax.experimental import pallas as pl
from jax.experimental.pallas import tpu as pltpu
from jax.sharding import Mesh, PartitionSpec as P

SIZES = (4, 4, 4, 4, 2, 2)
NAMES = ("zo", "zi", "x", "y", "h", "c")
LANES = 128

bf16 = jnp.bfloat16
f32 = jnp.float32
VMEM = 20 << 20


def column(y, h, c):
    return y * 4 + h * 2 + c


def pack_kernel(place_ref, near_ref, far_ref, packed_ref):
    packed_ref[:, :LANES] = near_ref[...]
    packed_ref[:, LANES:] = far_ref[...]


def pack(place, weight, n_y):
    depth, width = weight.shape
    return pl.pallas_call(
        pack_kernel,
        out_shape=jax.ShapeDtypeStruct((depth, width // 2), bf16),
        grid_spec=pltpu.PrefetchScalarGridSpec(
            num_scalar_prefetch=1,
            grid=(n_y,),
            in_specs=[
                pl.BlockSpec((depth, LANES), lambda y, p: (0, column((y + p[2]) % n_y, p[0], 1 - p[1]))),
                pl.BlockSpec((depth, LANES), lambda y, p: (0, column((y + p[2]) % n_y, 1 - p[0], 1 - p[1]))),
            ],
            out_specs=pl.BlockSpec((depth, 2 * LANES), lambda y, _: (0, y)),
        ),
        cost_estimate=pl.CostEstimate(flops=0, bytes_accessed=weight.size * 2, transcendentals=0),
        compiler_params=pltpu.CompilerParams(vmem_limit_bytes=VMEM),
    )(place, weight, weight)


def project_kernel(place_ref, own_ref, sibling_ref, near_ref, far_ref, packed_ref, *out_refs):
    mine = jnp.concatenate([near_ref[...], far_ref[...]], axis=1)
    total = jnp.dot(own_ref[...], mine, preferred_element_type=f32)
    total += jnp.dot(sibling_ref[...], packed_ref[...], preferred_element_type=f32)
    total = total.astype(bf16)
    for step, out_ref in enumerate(out_refs):

        @pl.when(pl.program_id(0) == step)
        def _(out_ref=out_ref):
            out_ref[...] = total


def project(place, own, sibling, weight, packed, n_y):
    rows, depth = own.shape
    width = weight.shape[1]
    return pl.pallas_call(
        project_kernel,
        out_shape=[jax.ShapeDtypeStruct((rows, 2 * LANES), bf16)] * n_y,
        grid_spec=pltpu.PrefetchScalarGridSpec(
            num_scalar_prefetch=1,
            grid=(n_y,),
            in_specs=[
                pl.BlockSpec((rows, depth), lambda y, _: (0, 0)),
                pl.BlockSpec((rows, depth), lambda y, _: (0, 0)),
                pl.BlockSpec((depth, LANES), lambda y, p: (0, column((y + p[2]) % n_y, p[0], p[1]))),
                pl.BlockSpec((depth, LANES), lambda y, p: (0, column((y + p[2]) % n_y, 1 - p[0], p[1]))),
                pl.BlockSpec((depth, 2 * LANES), lambda y, _: (0, y)),
            ],
            out_specs=[pl.BlockSpec((rows, 2 * LANES), lambda y, _: (0, 0))] * n_y,
        ),
        cost_estimate=pl.CostEstimate(
            flops=2 * rows * depth * width, bytes_accessed=rows * (4 * depth + width) + weight.size * 2, transcendentals=0
        ),
        compiler_params=pltpu.CompilerParams(vmem_limit_bytes=VMEM),
    )(place, own, sibling, weight, weight, packed)


def after(array, *earlier):
    return lax.optimization_barrier((array, *earlier))[0]


def shift(axis, size, step):
    return [(i, (i + step) % size) for i in range(size)]


def exchange(array, axis):
    return lax.all_to_all(array, axis, split_axis=0, concat_axis=0, tiled=True)


def gather_small(array, axis, size):
    return exchange(jnp.broadcast_to(array, (size, *array.shape)), axis)


def shards(local_weights, base, momentum, tokens, weight):
    sizes = dict(zip(NAMES, SIZES))
    zo, zi, x, y, h, c = (lax.axis_index(a) for a in NAMES)
    n_zo, n_zi, n_x, n_y = (sizes[a] for a in ("zo", "zi", "x", "y"))
    swap = [(0, 1), (1, 0)]
    groups = n_zo * n_zi * n_x
    rows, width = base.shape
    own = rows // groups
    per_x, per_zi = rows // n_x, rows // (n_x * n_zi)

    terms = exchange(local_weights[0].reshape(n_x, per_x, width), "x")

    place = jnp.stack([h, c, y]).astype(jnp.int32)
    sibling = lax.ppermute(tokens, "c", swap)
    packed = lax.ppermute(pack(place, weight, n_y), "c", swap)
    part = project(place, tokens, sibling, weight, packed, n_y)

    terms = after(terms, *part)
    anchor = lax.dynamic_slice_in_dim(base, x * per_x, per_x, 0).astype(bf16).astype(f32)
    total = (terms.astype(f32).sum(axis=0) - n_x * anchor).astype(bf16)

    pieces = [lax.ppermute(part[step], "y", shift("y", n_y, step)) for step in range(1, n_y)]

    def over_z(total):
        terms = exchange(total.reshape(n_zi, per_zi, width), "zi")
        total = terms.astype(f32).sum(axis=0).astype(bf16)
        terms = exchange(total.reshape(n_zo, own, width), "zo")
        outer_grad = (-terms.astype(f32).sum(axis=0) / groups).astype(bf16)
        gathered = gather_small(outer_grad, "zo", n_zo).reshape(per_zi, width)
        return gather_small(gathered, "zi", n_zi).reshape(per_x, width)

    outer_grad = lax.fori_loop(0, 1 + (h >> 4), lambda _, value: over_z(value), total)

    pieces = lax.optimization_barrier((outer_grad, *pieces))[1:]
    total = part[0].astype(f32)
    for piece in pieces:
        total += piece.astype(f32)
    mine, other = total[:, :LANES], total[:, LANES:].astype(bf16)
    mine, other = lax.optimization_barrier((mine, other))
    outer_grad = after(outer_grad, other)
    there = lax.ppermute(other, "h", swap)
    outer_grad = lax.all_gather(outer_grad, "x", axis=0, tiled=True).astype(f32)

    def step(outer_grad, base, momentum):
        new_momentum = 0.9 * momentum + outer_grad
        return base - 0.7 * (outer_grad + 0.9 * new_momentum), new_momentum

    synced = step(outer_grad, base, momentum)[0].astype(bf16)
    start = ((zo * n_zi + zi) * n_x + x) * own
    new_base, new_momentum = step(
        *(lax.dynamic_slice_in_dim(a, start, own, 0) for a in (outer_grad, base, momentum))
    )
    there = after(there, synced, new_base)
    keys_values = (mine + there.astype(f32)).astype(bf16)
    return new_base, new_momentum, synced, keys_values


def solution(mesh):
    fine = Mesh(mesh.devices.reshape(SIZES), NAMES)
    replica, mp = NAMES[:3], NAMES[3:]
    return jax.shard_map(
        shards,
        mesh=fine,
        in_specs=(
            P(replica, None, mp),
            P(None, mp),
            P(None, mp),
            P(replica, mp),
            P(mp, None),
        ),
        out_specs=(P(replica, mp), P(replica, mp), P(None, mp), P(replica, mp)),
        check_vma=False,
    )
```

```python
import jax
import jax.numpy as jnp
from jax import lax
from jax.experimental import pallas as pl
from jax.experimental.pallas import tpu as pltpu
from jax.sharding import Mesh, PartitionSpec as P

SIZES = (4, 4, 4, 4, 2, 2)
NAMES = ("zo", "zi", "x", "y", "h", "c")
LANES = 128

bf16 = jnp.bfloat16
f32 = jnp.float32
VMEM = 20 << 20


def column(y, h, c):
    return y * 4 + h * 2 + c


def pack_kernel(place_ref, near_ref, far_ref, packed_ref):
    packed_ref[:, :LANES] = near_ref[...]
    packed_ref[:, LANES:] = far_ref[...]


def pack(place, weight, n_y):
    depth, width = weight.shape
    return pl.pallas_call(
        pack_kernel,
        out_shape=jax.ShapeDtypeStruct((depth, width // 2), bf16),
        grid_spec=pltpu.PrefetchScalarGridSpec(
            num_scalar_prefetch=1,
            grid=(n_y,),
            in_specs=[
                pl.BlockSpec((depth, LANES), lambda y, p: (0, column((y + p[2]) % n_y, p[0], 1 - p[1]))),
                pl.BlockSpec((depth, LANES), lambda y, p: (0, column((y + p[2]) % n_y, 1 - p[0], 1 - p[1]))),
            ],
            out_specs=pl.BlockSpec((depth, 2 * LANES), lambda y, _: (0, y)),
        ),
        cost_estimate=pl.CostEstimate(flops=0, bytes_accessed=weight.size * 2, transcendentals=0),
        compiler_params=pltpu.CompilerParams(vmem_limit_bytes=VMEM),
    )(place, weight, weight)


def project_kernel(place_ref, own_ref, sibling_ref, near_ref, far_ref, packed_ref, *out_refs):
    mine = jnp.concatenate([near_ref[...], far_ref[...]], axis=1)
    total = jnp.dot(own_ref[...], mine, preferred_element_type=f32)
    total += jnp.dot(sibling_ref[...], packed_ref[...], preferred_element_type=f32)
    total = total.astype(bf16)
    for step, out_ref in enumerate(out_refs):

        @pl.when(pl.program_id(0) == step)
        def _(out_ref=out_ref):
            out_ref[...] = total


def project(place, own, sibling, weight, packed, n_y):
    rows, depth = own.shape
    width = weight.shape[1]
    return pl.pallas_call(
        project_kernel,
        out_shape=[jax.ShapeDtypeStruct((rows, 2 * LANES), bf16)] * n_y,
        grid_spec=pltpu.PrefetchScalarGridSpec(
            num_scalar_prefetch=1,
            grid=(n_y,),
            in_specs=[
                pl.BlockSpec((rows, depth), lambda y, _: (0, 0)),
                pl.BlockSpec((rows, depth), lambda y, _: (0, 0)),
                pl.BlockSpec((depth, LANES), lambda y, p: (0, column((y + p[2]) % n_y, p[0], p[1]))),
                pl.BlockSpec((depth, LANES), lambda y, p: (0, column((y + p[2]) % n_y, 1 - p[0], p[1]))),
                pl.BlockSpec((depth, 2 * LANES), lambda y, _: (0, y)),
            ],
            out_specs=[pl.BlockSpec((rows, 2 * LANES), lambda y, _: (0, 0))] * n_y,
        ),
        cost_estimate=pl.CostEstimate(
            flops=2 * rows * depth * width, bytes_accessed=rows * (4 * depth + width) + weight.size * 2, transcendentals=0
        ),
        compiler_params=pltpu.CompilerParams(vmem_limit_bytes=VMEM),
    )(place, own, sibling, weight, weight, packed)


def after(array, *earlier):
    return lax.optimization_barrier((array, *earlier))[0]


def shift(axis, size, step):
    return [(i, (i + step) % size) for i in range(size)]


def exchange(array, axis):
    return lax.all_to_all(array, axis, split_axis=0, concat_axis=0, tiled=True)


def gather_small(array, axis, size):
    return exchange(jnp.broadcast_to(array, (size, *array.shape)), axis)


def shards(local_weights, base, momentum, tokens, weight):
    sizes = dict(zip(NAMES, SIZES))
    zo, zi, x, y, h, c = (lax.axis_index(a) for a in NAMES)
    n_zo, n_zi, n_x, n_y = (sizes[a] for a in ("zo", "zi", "x", "y"))
    swap = [(0, 1), (1, 0)]
    groups = n_zo * n_zi * n_x
    rows, width = base.shape
    own = rows // groups
    per_x, per_zi = rows // n_x, rows // (n_x * n_zi)

    terms = exchange(local_weights[0].reshape(n_x, per_x, width), "x")

    place = jnp.stack([h, c, y]).astype(jnp.int32)
    sibling = lax.ppermute(tokens, "c", swap)
    packed = lax.ppermute(pack(place, weight, n_y), "c", swap)
    part = project(place, tokens, sibling, weight, packed, n_y)

    terms = after(terms, *part)
    anchor = lax.dynamic_slice_in_dim(base, x * per_x, per_x, 0).astype(bf16).astype(f32)
    total = (terms.astype(f32).sum(axis=0) - n_x * anchor).astype(bf16)

    part = [part[0]] + [lax.ppermute(part[step], "y", shift("y", n_y, step)) for step in range(1, n_y)]

    once = 1 + (h >> 4)

    def over_zi(total):
        terms = exchange(total.reshape(n_zi, per_zi, width), "zi")
        return terms.astype(f32).sum(axis=0).astype(bf16)

    empty = jnp.zeros((per_zi, width), bf16)
    total = lax.fori_loop(0, once, lambda _, carry: (carry[0] + carry[0], over_zi(carry[0])), (total, empty))[1]

    total, *part = lax.optimization_barrier((total, *part))

    terms = gather_small(total, "zo", n_zo)

    kv = part[0].astype(f32)
    for piece in part[1:]:
        kv += piece.astype(f32)
    mine, other = lax.optimization_barrier((kv[:, :LANES], kv[:, LANES:].astype(bf16)))
    there = lax.ppermute(other, "h", swap)

    terms = after(terms, other)
    outer_grad = (-terms.astype(f32).sum(axis=0) / groups).astype(bf16)

    def over_zi_and_x(outer_grad):
        gathered = gather_small(outer_grad, "zi", n_zi).reshape(per_x, width)
        return lax.all_gather(gathered, "x", axis=0, tiled=True)

    empty = jnp.zeros((rows, width), bf16)
    outer_grad = lax.fori_loop(
        0, once, lambda _, carry: (carry[0] + carry[0], over_zi_and_x(carry[0])), (outer_grad, empty)
    )[1].astype(f32)

    def step(outer_grad, base, momentum):
        new_momentum = 0.9 * momentum + outer_grad
        return base - 0.7 * (outer_grad + 0.9 * new_momentum), new_momentum

    synced = step(outer_grad, base, momentum)[0].astype(bf16)
    start = ((zo * n_zi + zi) * n_x + x) * own
    new_base, new_momentum = step(
        *(lax.dynamic_slice_in_dim(a, start, own, 0) for a in (outer_grad, base, momentum))
    )
    there = after(there, synced, new_base)
    keys_values = (mine + there.astype(f32)).astype(bf16)
    return new_base, new_momentum, synced, keys_values


def solution(mesh):
    fine = Mesh(mesh.devices.reshape(SIZES), NAMES)
    replica, mp = NAMES[:3], NAMES[3:]
    return jax.shard_map(
        shards,
        mesh=fine,
        in_specs=(
            P(replica, None, mp),
            P(None, mp),
            P(None, mp),
            P(replica, mp),
            P(mp, None),
        ),
        out_specs=(P(replica, mp), P(replica, mp), P(None, mp), P(replica, mp)),
        check_vma=False,
    )
```

```python
import jax
import jax.numpy as jnp
from jax import lax
from jax.experimental import pallas as pl
from jax.experimental.pallas import tpu as pltpu
from jax.sharding import Mesh, PartitionSpec as P

SIZES = (4, 4, 4, 4, 2, 2)
NAMES = ("zo", "zi", "x", "y", "h", "c")
LANES = 128

bf16 = jnp.bfloat16
f32 = jnp.float32
VMEM = 20 << 20


def column(y, h, c):
    return y * 4 + h * 2 + c


def pack_kernel(place_ref, near_ref, far_ref, packed_ref):
    packed_ref[:, :LANES] = near_ref[...]
    packed_ref[:, LANES:] = far_ref[...]


def pack(place, weight, n_y):
    depth, width = weight.shape
    return pl.pallas_call(
        pack_kernel,
        out_shape=jax.ShapeDtypeStruct((depth, width // 2), bf16),
        grid_spec=pltpu.PrefetchScalarGridSpec(
            num_scalar_prefetch=1,
            grid=(n_y,),
            in_specs=[
                pl.BlockSpec((depth, LANES), lambda y, p: (0, column((y + p[2]) % n_y, p[0], 1 - p[1]))),
                pl.BlockSpec((depth, LANES), lambda y, p: (0, column((y + p[2]) % n_y, 1 - p[0], 1 - p[1]))),
            ],
            out_specs=pl.BlockSpec((depth, 2 * LANES), lambda y, _: (0, y)),
        ),
        cost_estimate=pl.CostEstimate(flops=0, bytes_accessed=weight.size * 2, transcendentals=0),
        compiler_params=pltpu.CompilerParams(vmem_limit_bytes=VMEM),
    )(place, weight, weight)


def project_kernel(place_ref, own_ref, sibling_ref, near_ref, far_ref, packed_ref, *out_refs):
    mine = jnp.concatenate([near_ref[...], far_ref[...]], axis=1)
    total = jnp.dot(own_ref[...], mine, preferred_element_type=f32)
    total += jnp.dot(sibling_ref[...], packed_ref[...], preferred_element_type=f32)
    total = total.astype(bf16)
    for step, out_ref in enumerate(out_refs):

        @pl.when(pl.program_id(0) == step)
        def _(out_ref=out_ref):
            out_ref[...] = total


def project(place, own, sibling, weight, packed, n_y):
    rows, depth = own.shape
    width = weight.shape[1]
    return pl.pallas_call(
        project_kernel,
        out_shape=[jax.ShapeDtypeStruct((rows, 2 * LANES), bf16)] * n_y,
        grid_spec=pltpu.PrefetchScalarGridSpec(
            num_scalar_prefetch=1,
            grid=(n_y,),
            in_specs=[
                pl.BlockSpec((rows, depth), lambda y, _: (0, 0)),
                pl.BlockSpec((rows, depth), lambda y, _: (0, 0)),
                pl.BlockSpec((depth, LANES), lambda y, p: (0, column((y + p[2]) % n_y, p[0], p[1]))),
                pl.BlockSpec((depth, LANES), lambda y, p: (0, column((y + p[2]) % n_y, 1 - p[0], p[1]))),
                pl.BlockSpec((depth, 2 * LANES), lambda y, _: (0, y)),
            ],
            out_specs=[pl.BlockSpec((rows, 2 * LANES), lambda y, _: (0, 0))] * n_y,
        ),
        cost_estimate=pl.CostEstimate(
            flops=2 * rows * depth * width, bytes_accessed=rows * (4 * depth + width) + weight.size * 2, transcendentals=0
        ),
        compiler_params=pltpu.CompilerParams(vmem_limit_bytes=VMEM),
    )(place, own, sibling, weight, weight, packed)


def after(array, *earlier):
    return lax.optimization_barrier((array, *earlier))[0]


def shift(axis, size, step):
    return [(i, (i + step) % size) for i in range(size)]


def exchange(array, axis):
    return lax.all_to_all(array, axis, split_axis=0, concat_axis=0, tiled=True)


def gather_small(array, axis, size):
    return exchange(jnp.broadcast_to(array, (size, *array.shape)), axis)


def shards(local_weights, base, momentum, tokens, weight):
    sizes = dict(zip(NAMES, SIZES))
    zo, zi, x, y, h, c = (lax.axis_index(a) for a in NAMES)
    n_zo, n_zi, n_x, n_y = (sizes[a] for a in ("zo", "zi", "x", "y"))
    swap = [(0, 1), (1, 0)]
    groups = n_zo * n_zi * n_x
    rows, width = base.shape
    own = rows // groups
    per_x, per_zi = rows // n_x, rows // (n_x * n_zi)

    terms = exchange(local_weights[0].reshape(n_x, per_x, width), "x")
    anchor = lax.dynamic_slice_in_dim(base, x * per_x, per_x, 0).astype(bf16).astype(f32)
    total = (terms.astype(f32).sum(axis=0) - n_x * anchor).astype(bf16)

    place = jnp.stack([h, c, y]).astype(jnp.int32)
    sibling = lax.ppermute(tokens, "c", swap)
    packed = lax.ppermute(pack(place, weight, n_y), "c", swap)

    total, sibling, packed = lax.optimization_barrier((total, sibling, packed))
    terms = exchange(total.reshape(n_zi, per_zi, width), "zi")
    part = project(place, tokens, sibling, weight, packed, n_y)
    terms = after(terms, *part)
    total = terms.astype(f32).sum(axis=0).astype(bf16)
    total, *part = lax.optimization_barrier((total, *part))
    part = [part[0]] + [lax.ppermute(part[step], "y", shift("y", n_y, step)) for step in range(1, n_y)]

    once = 1 + (h >> 4)

    def alone(function, value, shape):
        carry = (value, jnp.zeros(shape, bf16))
        return lax.fori_loop(0, once, lambda _, carry: (-carry[0], function(carry[0])), carry)[1]

    def over_zo(total):
        terms = gather_small(total, "zo", n_zo)
        return (-terms.astype(f32).sum(axis=0) / groups).astype(bf16)

    outer_grad = alone(over_zo, total, (per_zi, width))
    outer_grad, *part = lax.optimization_barrier((outer_grad, *part))
    gathered = gather_small(outer_grad, "zi", n_zi)

    kv = part[0].astype(f32)
    for piece in part[1:]:
        kv += piece.astype(f32)
    mine, other = lax.optimization_barrier((kv[:, :LANES], kv[:, LANES:].astype(bf16)))
    there = lax.ppermute(other, "h", swap)

    gathered = after(gathered, other).reshape(per_x, width)
    outer_grad = alone(lambda value: lax.all_gather(value, "x", axis=0, tiled=True), gathered, (rows, width))
    outer_grad = outer_grad.astype(f32)

    def step(outer_grad, base, momentum):
        new_momentum = 0.9 * momentum + outer_grad
        return base - 0.7 * (outer_grad + 0.9 * new_momentum), new_momentum

    synced = step(outer_grad, base, momentum)[0].astype(bf16)
    start = ((zo * n_zi + zi) * n_x + x) * own
    new_base, new_momentum = step(
        *(lax.dynamic_slice_in_dim(a, start, own, 0) for a in (outer_grad, base, momentum))
    )
    there = after(there, synced, new_base)
    keys_values = (mine + there.astype(f32)).astype(bf16)
    return new_base, new_momentum, synced, keys_values


def solution(mesh):
    fine = Mesh(mesh.devices.reshape(SIZES), NAMES)
    replica, mp = NAMES[:3], NAMES[3:]
    return jax.shard_map(
        shards,
        mesh=fine,
        in_specs=(
            P(replica, None, mp),
            P(None, mp),
            P(None, mp),
            P(replica, mp),
            P(mp, None),
        ),
        out_specs=(P(replica, mp), P(replica, mp), P(None, mp), P(replica, mp)),
        check_vma=False,
    )
```

```python
import jax
import jax.numpy as jnp
from jax import lax
from jax.experimental import pallas as pl
from jax.experimental.pallas import tpu as pltpu
from jax.sharding import Mesh, PartitionSpec as P

SIZES = (2, 8, 4, 4, 2, 2)
NAMES = ("zo", "zi", "x", "y", "h", "c")
LANES = 128

bf16 = jnp.bfloat16
f32 = jnp.float32
VMEM = 20 << 20


def column(y, h, c):
    return y * 4 + h * 2 + c


def pack_kernel(place_ref, near_ref, far_ref, packed_ref):
    packed_ref[:, :LANES] = near_ref[...]
    packed_ref[:, LANES:] = far_ref[...]


def pack(place, weight, n_y):
    depth, width = weight.shape
    return pl.pallas_call(
        pack_kernel,
        out_shape=jax.ShapeDtypeStruct((depth, width // 2), bf16),
        grid_spec=pltpu.PrefetchScalarGridSpec(
            num_scalar_prefetch=1,
            grid=(n_y,),
            in_specs=[
                pl.BlockSpec((depth, LANES), lambda y, p: (0, column((y + p[2]) % n_y, p[0], 1 - p[1]))),
                pl.BlockSpec((depth, LANES), lambda y, p: (0, column((y + p[2]) % n_y, 1 - p[0], 1 - p[1]))),
            ],
            out_specs=pl.BlockSpec((depth, 2 * LANES), lambda y, _: (0, y)),
        ),
        cost_estimate=pl.CostEstimate(flops=0, bytes_accessed=weight.size * 2, transcendentals=0),
        compiler_params=pltpu.CompilerParams(vmem_limit_bytes=VMEM),
    )(place, weight, weight)


def project_kernel(place_ref, own_ref, sibling_ref, near_ref, far_ref, packed_ref, *out_refs):
    mine = jnp.concatenate([near_ref[...], far_ref[...]], axis=1)
    total = jnp.dot(own_ref[...], mine, preferred_element_type=f32)
    total += jnp.dot(sibling_ref[...], packed_ref[...], preferred_element_type=f32)
    total = total.astype(bf16)
    for step, out_ref in enumerate(out_refs):

        @pl.when(pl.program_id(0) == step)
        def _(out_ref=out_ref):
            out_ref[...] = total


def project(place, own, sibling, weight, packed, n_y):
    rows, depth = own.shape
    width = weight.shape[1]
    return pl.pallas_call(
        project_kernel,
        out_shape=[jax.ShapeDtypeStruct((rows, 2 * LANES), bf16)] * n_y,
        grid_spec=pltpu.PrefetchScalarGridSpec(
            num_scalar_prefetch=1,
            grid=(n_y,),
            in_specs=[
                pl.BlockSpec((rows, depth), lambda y, _: (0, 0)),
                pl.BlockSpec((rows, depth), lambda y, _: (0, 0)),
                pl.BlockSpec((depth, LANES), lambda y, p: (0, column((y + p[2]) % n_y, p[0], p[1]))),
                pl.BlockSpec((depth, LANES), lambda y, p: (0, column((y + p[2]) % n_y, 1 - p[0], p[1]))),
                pl.BlockSpec((depth, 2 * LANES), lambda y, _: (0, y)),
            ],
            out_specs=[pl.BlockSpec((rows, 2 * LANES), lambda y, _: (0, 0))] * n_y,
        ),
        cost_estimate=pl.CostEstimate(
            flops=2 * rows * depth * width, bytes_accessed=rows * (4 * depth + width) + weight.size * 2, transcendentals=0
        ),
        compiler_params=pltpu.CompilerParams(vmem_limit_bytes=VMEM),
    )(place, own, sibling, weight, weight, packed)


def after(array, *earlier):
    return lax.optimization_barrier((array, *earlier))[0]


def shift(axis, size, step):
    return [(i, (i + step) % size) for i in range(size)]


def exchange(array, axis):
    return lax.all_to_all(array, axis, split_axis=0, concat_axis=0, tiled=True)


def gather_small(array, axis, size):
    return exchange(jnp.broadcast_to(array, (size, *array.shape)), axis)


def shards(local_weights, base, momentum, tokens, weight):
    sizes = dict(zip(NAMES, SIZES))
    zo, zi, x, y, h, c = (lax.axis_index(a) for a in NAMES)
    n_zo, n_zi, n_x, n_y = (sizes[a] for a in ("zo", "zi", "x", "y"))
    swap = [(0, 1), (1, 0)]
    groups = n_zo * n_zi * n_x
    rows, width = base.shape
    own = rows // groups
    per_x, per_zi = rows // n_x, rows // (n_x * n_zi)

    terms = exchange(local_weights[0].reshape(n_x, per_x, width), "x")

    place = jnp.stack([h, c, y]).astype(jnp.int32)
    sibling = lax.ppermute(tokens, "c", swap)
    packed = lax.ppermute(pack(place, weight, n_y), "c", swap)
    part = project(place, tokens, sibling, weight, packed, n_y)

    terms = after(terms, *part)
    anchor = lax.dynamic_slice_in_dim(base, x * per_x, per_x, 0).astype(bf16).astype(f32)
    total = (terms.astype(f32).sum(axis=0) - n_x * anchor).astype(bf16)
    part = [part[0]] + [lax.ppermute(part[step], "y", shift("y", n_y, step)) for step in range(1, n_y)]

    once = 1 + (h >> 4)

    def alone(function, value, shape):
        carry = (value, jnp.zeros(shape, bf16))
        return lax.fori_loop(0, once, lambda _, carry: (-carry[0], function(carry[0])), carry)[1]

    def over_zi(total):
        terms = exchange(total.reshape(n_zi, per_zi, width), "zi")
        return terms.astype(f32).sum(axis=0).astype(bf16)

    total = alone(over_zi, total, (per_zi, width))
    total, *part = lax.optimization_barrier((total, *part))

    across = lax.ppermute(total, "zo", swap)
    kv = part[0].astype(f32)
    for piece in part[1:]:
        kv += piece.astype(f32)
    mine, other = lax.optimization_barrier((kv[:, :LANES], kv[:, LANES:].astype(bf16)))
    across = after(across, other)
    outer_grad = (-(total.astype(f32) + across.astype(f32)) / groups).astype(bf16)
    outer_grad, other = lax.optimization_barrier((outer_grad, other))

    gathered = gather_small(outer_grad, "zi", n_zi)
    there = lax.ppermute(other, "h", swap)

    gathered = after(gathered, other).reshape(per_x, width)
    outer_grad = alone(lambda value: lax.all_gather(value, "x", axis=0, tiled=True), gathered, (rows, width))
    outer_grad = outer_grad.astype(f32)

    def step(outer_grad, base, momentum):
        new_momentum = 0.9 * momentum + outer_grad
        return base - 0.7 * (outer_grad + 0.9 * new_momentum), new_momentum

    synced = step(outer_grad, base, momentum)[0].astype(bf16)
    start = ((zo * n_zi + zi) * n_x + x) * own
    new_base, new_momentum = step(
        *(lax.dynamic_slice_in_dim(a, start, own, 0) for a in (outer_grad, base, momentum))
    )
    there = after(there, synced, new_base)
    keys_values = (mine + there.astype(f32)).astype(bf16)
    return new_base, new_momentum, synced, keys_values


def solution(mesh):
    fine = Mesh(mesh.devices.reshape(SIZES), NAMES)
    replica, mp = NAMES[:3], NAMES[3:]
    return jax.shard_map(
        shards,
        mesh=fine,
        in_specs=(
            P(replica, None, mp),
            P(None, mp),
            P(None, mp),
            P(replica, mp),
            P(mp, None),
        ),
        out_specs=(P(replica, mp), P(replica, mp), P(None, mp), P(replica, mp)),
        check_vma=False,
    )
```

```python
import jax
import jax.numpy as jnp
from jax import lax
from jax.experimental import pallas as pl
from jax.experimental.pallas import tpu as pltpu
from jax.sharding import Mesh, PartitionSpec as P

SIZES = (2, 8, 4, 4, 2, 2)
NAMES = ("zo", "zi", "x", "y", "h", "c")
LANES = 128

bf16 = jnp.bfloat16
f32 = jnp.float32
VMEM = 20 << 20


def column(y, h, c):
    return y * 4 + h * 2 + c


def pack_kernel(place_ref, near_ref, far_ref, packed_ref):
    packed_ref[:, :LANES] = near_ref[...]
    packed_ref[:, LANES:] = far_ref[...]


def pack(place, weight, n_y):
    depth, width = weight.shape
    return pl.pallas_call(
        pack_kernel,
        out_shape=jax.ShapeDtypeStruct((depth, width // 2), bf16),
        grid_spec=pltpu.PrefetchScalarGridSpec(
            num_scalar_prefetch=1,
            grid=(n_y,),
            in_specs=[
                pl.BlockSpec((depth, LANES), lambda y, p: (0, column((y + p[2]) % n_y, p[0], 1 - p[1]))),
                pl.BlockSpec((depth, LANES), lambda y, p: (0, column((y + p[2]) % n_y, 1 - p[0], 1 - p[1]))),
            ],
            out_specs=pl.BlockSpec((depth, 2 * LANES), lambda y, _: (0, y)),
        ),
        cost_estimate=pl.CostEstimate(flops=0, bytes_accessed=weight.size * 2, transcendentals=0),
        compiler_params=pltpu.CompilerParams(vmem_limit_bytes=VMEM),
    )(place, weight, weight)


def project_kernel(place_ref, own_ref, sibling_ref, near_ref, far_ref, packed_ref, *out_refs):
    mine = jnp.concatenate([near_ref[...], far_ref[...]], axis=1)
    total = jnp.dot(own_ref[...], mine, preferred_element_type=f32)
    total += jnp.dot(sibling_ref[...], packed_ref[...], preferred_element_type=f32)
    total = total.astype(bf16)
    for step, out_ref in enumerate(out_refs):

        @pl.when(pl.program_id(0) == step)
        def _(out_ref=out_ref):
            out_ref[...] = total


def project(place, own, sibling, weight, packed, n_y):
    rows, depth = own.shape
    width = weight.shape[1]
    return pl.pallas_call(
        project_kernel,
        out_shape=[jax.ShapeDtypeStruct((rows, 2 * LANES), bf16)] * n_y,
        grid_spec=pltpu.PrefetchScalarGridSpec(
            num_scalar_prefetch=1,
            grid=(n_y,),
            in_specs=[
                pl.BlockSpec((rows, depth), lambda y, _: (0, 0)),
                pl.BlockSpec((rows, depth), lambda y, _: (0, 0)),
                pl.BlockSpec((depth, LANES), lambda y, p: (0, column((y + p[2]) % n_y, p[0], p[1]))),
                pl.BlockSpec((depth, LANES), lambda y, p: (0, column((y + p[2]) % n_y, 1 - p[0], p[1]))),
                pl.BlockSpec((depth, 2 * LANES), lambda y, _: (0, y)),
            ],
            out_specs=[pl.BlockSpec((rows, 2 * LANES), lambda y, _: (0, 0))] * n_y,
        ),
        cost_estimate=pl.CostEstimate(
            flops=2 * rows * depth * width, bytes_accessed=rows * (4 * depth + width) + weight.size * 2, transcendentals=0
        ),
        compiler_params=pltpu.CompilerParams(vmem_limit_bytes=VMEM),
    )(place, own, sibling, weight, weight, packed)


def after(array, *earlier):
    return lax.optimization_barrier((array, *earlier))[0]


def shift(axis, size, step):
    return [(i, (i + step) % size) for i in range(size)]


def exchange(array, axis):
    return lax.all_to_all(array, axis, split_axis=0, concat_axis=0, tiled=True)


def gather_small(array, axis, size):
    return exchange(jnp.broadcast_to(array, (size, *array.shape)), axis)


def shards(local_weights, base, momentum, tokens, weight):
    sizes = dict(zip(NAMES, SIZES))
    zo, zi, x, y, h, c = (lax.axis_index(a) for a in NAMES)
    n_zo, n_zi, n_x, n_y = (sizes[a] for a in ("zo", "zi", "x", "y"))
    swap = [(0, 1), (1, 0)]
    groups = n_zo * n_zi * n_x
    rows, width = base.shape
    own = rows // groups
    per_x, per_zi = rows // n_x, rows // (n_x * n_zi)

    terms = exchange(local_weights[0].reshape(n_x, per_x, width), "x")

    anchor = lax.dynamic_slice_in_dim(base, x * per_x, per_x, 0).astype(bf16).astype(f32)
    total = (terms.astype(f32).sum(axis=0) - n_x * anchor).astype(bf16)

    place = jnp.stack([h, c, y]).astype(jnp.int32)
    sibling = lax.ppermute(tokens, "c", swap)
    packed = lax.ppermute(pack(place, weight, n_y), "c", swap)

    total, sibling, packed = lax.optimization_barrier((total, sibling, packed))
    terms = exchange(total.reshape(n_zi, per_zi, width), "zi")
    part = project(place, tokens, sibling, weight, packed, n_y)
    terms = after(terms, *part)
    total = terms.astype(f32).sum(axis=0).astype(bf16)
    total, *part = lax.optimization_barrier((total, *part))
    part = [part[0]] + [lax.ppermute(part[step], "y", shift("y", n_y, step)) for step in range(1, n_y)]

    once = 1 + (h >> 4)

    def alone(function, value, shape):
        carry = (value, jnp.zeros(shape, bf16))
        return lax.fori_loop(0, once, lambda _, carry: (-carry[0], function(carry[0])), carry)[1]

    def outer(total):
        across = lax.ppermute(total, "zo", swap)
        return (-(total.astype(f32) + across.astype(f32)) / groups).astype(bf16)

    outer_grad = alone(outer, total, (per_zi, width))
    outer_grad, base, momentum, *part = lax.optimization_barrier((outer_grad, base, momentum, *part))
    gathered = gather_small(outer_grad, "zi", n_zi)

    kv = part[0].astype(f32)
    for piece in part[1:]:
        kv += piece.astype(f32)
    without = base - 0.567 * momentum
    mine, other, without = lax.optimization_barrier((kv[:, :LANES], kv[:, LANES:].astype(bf16), without))
    there = lax.ppermute(other, "h", swap)

    gathered = after(gathered, other).reshape(per_x, width)
    outer_grad = alone(lambda value: lax.all_gather(value, "x", axis=0, tiled=True), gathered, (rows, width))

    synced = (without - 1.33 * outer_grad.astype(f32)).astype(bf16)
    start = ((zo * n_zi + zi) * n_x + x) * own

    def own_rows(array):
        return lax.dynamic_slice_in_dim(array, start, own, 0).astype(f32)

    new_base = own_rows(without) - 1.33 * own_rows(outer_grad)
    new_momentum = 0.9 * own_rows(momentum) + own_rows(outer_grad)
    there = after(there, synced, new_base)
    keys_values = (mine + there.astype(f32)).astype(bf16)
    return new_base, new_momentum, synced, keys_values


def solution(mesh):
    fine = Mesh(mesh.devices.reshape(SIZES), NAMES)
    replica, mp = NAMES[:3], NAMES[3:]
    return jax.shard_map(
        shards,
        mesh=fine,
        in_specs=(
            P(replica, None, mp),
            P(None, mp),
            P(None, mp),
            P(replica, mp),
            P(mp, None),
        ),
        out_specs=(P(replica, mp), P(replica, mp), P(None, mp), P(replica, mp)),
        check_vma=False,
    )
```

```python
import jax
import jax.numpy as jnp
from jax import lax
from jax.experimental import pallas as pl
from jax.experimental.pallas import tpu as pltpu
from jax.sharding import Mesh, PartitionSpec as P

SIZES = (2, 8, 4, 4, 2, 2)
NAMES = ("zo", "zi", "x", "y", "h", "c")
LANES = 128

bf16 = jnp.bfloat16
f32 = jnp.float32
VMEM = 20 << 20


def column(y, h, c):
    return y * 4 + h * 2 + c


def pack_kernel(place_ref, near_ref, far_ref, packed_ref):
    packed_ref[:, :LANES] = near_ref[...]
    packed_ref[:, LANES:] = far_ref[...]


def pack(place, weight, n_y):
    depth, width = weight.shape
    return pl.pallas_call(
        pack_kernel,
        out_shape=jax.ShapeDtypeStruct((depth, width // 2), bf16),
        grid_spec=pltpu.PrefetchScalarGridSpec(
            num_scalar_prefetch=1,
            grid=(n_y,),
            in_specs=[
                pl.BlockSpec((depth, LANES), lambda y, p: (0, column(y, p[0], 1 - p[1]))),
                pl.BlockSpec((depth, LANES), lambda y, p: (0, column(y, 1 - p[0], 1 - p[1]))),
            ],
            out_specs=pl.BlockSpec((depth, 2 * LANES), lambda y, _: (0, y)),
        ),
        cost_estimate=pl.CostEstimate(flops=0, bytes_accessed=weight.size * 2, transcendentals=0),
        compiler_params=pltpu.CompilerParams(vmem_limit_bytes=VMEM),
    )(place, weight, weight)


def project_kernel(place_ref, own_ref, sibling_ref, near_ref, far_ref, packed_ref, out_ref):
    mine = jnp.concatenate([near_ref[...], far_ref[...]], axis=1)
    total = jnp.dot(own_ref[...], mine, preferred_element_type=f32)
    total += jnp.dot(sibling_ref[...], packed_ref[...], preferred_element_type=f32)
    out_ref[0] = total.astype(bf16)


def project(place, own, sibling, weight, packed, n_y):
    rows, depth = own.shape
    width = weight.shape[1]
    return pl.pallas_call(
        project_kernel,
        out_shape=jax.ShapeDtypeStruct((n_y, rows, 2 * LANES), bf16),
        grid_spec=pltpu.PrefetchScalarGridSpec(
            num_scalar_prefetch=1,
            grid=(n_y,),
            in_specs=[
                pl.BlockSpec((rows, depth), lambda y, _: (0, 0)),
                pl.BlockSpec((rows, depth), lambda y, _: (0, 0)),
                pl.BlockSpec((depth, LANES), lambda y, p: (0, column(y, p[0], p[1]))),
                pl.BlockSpec((depth, LANES), lambda y, p: (0, column(y, 1 - p[0], p[1]))),
                pl.BlockSpec((depth, 2 * LANES), lambda y, _: (0, y)),
            ],
            out_specs=pl.BlockSpec((1, rows, 2 * LANES), lambda y, _: (y, 0, 0)),
        ),
        cost_estimate=pl.CostEstimate(
            flops=2 * rows * depth * width, bytes_accessed=rows * (4 * depth + width) + weight.size * 2, transcendentals=0
        ),
        compiler_params=pltpu.CompilerParams(vmem_limit_bytes=VMEM),
    )(place, own, sibling, weight, weight, packed)


def after(array, *earlier):
    return lax.optimization_barrier((array, *earlier))[0]


def exchange(array, axis):
    return lax.all_to_all(array, axis, split_axis=0, concat_axis=0, tiled=True)


def shards(local_weights, base, momentum, tokens, weight):
    sizes = dict(zip(NAMES, SIZES))
    zo, zi, x, _, h, c = (lax.axis_index(a) for a in NAMES)
    n_zo, n_zi, n_x, n_y = (sizes[a] for a in ("zo", "zi", "x", "y"))
    swap = [(0, 1), (1, 0)]
    groups = n_zo * n_zi * n_x
    rows, width = base.shape
    own = rows // groups
    per_x, per_zi = rows // n_x, rows // (n_x * n_zi)

    terms = exchange(local_weights[0].reshape(n_x, per_x, width), "x")

    anchor = lax.dynamic_slice_in_dim(base, x * per_x, per_x, 0).astype(bf16).astype(f32)
    total = terms[0].astype(f32) - n_x * anchor
    for term in range(1, n_x):
        total += terms[term].astype(f32)
    total = total.astype(bf16)

    place = jnp.stack([h, c]).astype(jnp.int32)
    sibling = lax.ppermute(tokens, "c", swap)
    packed = lax.ppermute(pack(place, weight, n_y), "c", swap)

    total, sibling, packed = lax.optimization_barrier((total, sibling, packed))
    terms = exchange(total.reshape(n_zi, per_zi, width), "zi")
    part = project(place, tokens, sibling, weight, packed, n_y)
    terms = after(terms, part)
    total = terms.astype(f32).sum(axis=0).astype(bf16)
    total, part = lax.optimization_barrier((total, part))
    part = exchange(part, "y")

    once = 1 + (h >> 4)

    def alone(function, value, shape):
        carry = (value, jnp.zeros(shape, bf16))
        return lax.fori_loop(0, once, lambda _, carry: (-carry[0], function(carry[0])), carry)[1]

    def outer(total):
        across = lax.ppermute(total, "zo", swap)
        outer_grad = (-(total.astype(f32) + across.astype(f32)) / groups).astype(bf16)
        return jnp.broadcast_to(outer_grad, (n_zi, per_zi, width))

    outer_grad = alone(outer, total, (n_zi, per_zi, width))
    outer_grad, base, momentum, part = lax.optimization_barrier((outer_grad, base, momentum, part))
    gathered = exchange(outer_grad, "zi")

    kv = part[0].astype(f32)
    for piece in range(1, n_y):
        kv += part[piece].astype(f32)
    without = base - 0.567 * momentum
    mine, other, without = lax.optimization_barrier((kv[:, :LANES], kv[:, LANES:].astype(bf16), without))
    gathered, other = lax.optimization_barrier((gathered, other))
    there = lax.ppermute(other, "h", swap)
    gathered = gathered.reshape(per_x, width)
    start = ((zo * n_zi + zi) * n_x + x) * own

    def own_rows(array):
        return lax.dynamic_slice_in_dim(array, start, own, 0).astype(f32)

    def finish(gathered):
        outer_grad = lax.all_gather(gathered, "x", axis=0, tiled=True)
        synced = (without - 1.33 * outer_grad.astype(f32)).astype(bf16)
        new_base = own_rows(without) - 1.33 * own_rows(outer_grad)
        new_momentum = 0.9 * own_rows(momentum) + own_rows(outer_grad)
        return synced, new_base, new_momentum

    empty = (jnp.zeros((rows, width), bf16), jnp.zeros((own, width), f32), jnp.zeros((own, width), f32))
    carry = (gathered, *empty)
    carry = lax.fori_loop(0, once, lambda _, carry: (-carry[0], *finish(carry[0])), carry)
    synced, new_base, new_momentum = carry[1:]
    there = after(there, synced, new_base)
    keys_values = (mine + there.astype(f32)).astype(bf16)
    return new_base, new_momentum, synced, keys_values


def solution(mesh):
    fine = Mesh(mesh.devices.reshape(SIZES), NAMES)
    replica, mp = NAMES[:3], NAMES[3:]
    return jax.shard_map(
        shards,
        mesh=fine,
        in_specs=(
            P(replica, None, mp),
            P(None, mp),
            P(None, mp),
            P(replica, mp),
            P(mp, None),
        ),
        out_specs=(P(replica, mp), P(replica, mp), P(None, mp), P(replica, mp)),
        check_vma=False,
    )
```

```python
import jax
import jax.numpy as jnp
from jax import lax
from jax.experimental import pallas as pl
from jax.experimental.pallas import tpu as pltpu
from jax.sharding import Mesh, PartitionSpec as P

SIZES = (2, 8, 4, 4, 2, 2)
NAMES = ("zo", "zi", "x", "y", "h", "c")
LANES = 128

bf16 = jnp.bfloat16
f32 = jnp.float32
VMEM = 20 << 20


def column(y, h, c):
    return y * 4 + h * 2 + c


def pack_kernel(place_ref, near_ref, far_ref, packed_ref):
    packed_ref[:, :LANES] = near_ref[...]
    packed_ref[:, LANES:] = far_ref[...]


def pack(place, weight, n_y):
    depth, width = weight.shape
    return pl.pallas_call(
        pack_kernel,
        out_shape=jax.ShapeDtypeStruct((depth, width // 2), bf16),
        grid_spec=pltpu.PrefetchScalarGridSpec(
            num_scalar_prefetch=1,
            grid=(n_y,),
            in_specs=[
                pl.BlockSpec((depth, LANES), lambda y, p: (0, column((y + p[2]) % n_y, p[0], 1 - p[1]))),
                pl.BlockSpec((depth, LANES), lambda y, p: (0, column((y + p[2]) % n_y, 1 - p[0], 1 - p[1]))),
            ],
            out_specs=pl.BlockSpec((depth, 2 * LANES), lambda y, _: (0, y)),
        ),
        cost_estimate=pl.CostEstimate(flops=0, bytes_accessed=weight.size * 2, transcendentals=0),
        compiler_params=pltpu.CompilerParams(vmem_limit_bytes=VMEM),
    )(place, weight, weight)


def project_kernel(place_ref, own_ref, sibling_ref, near_ref, far_ref, packed_ref, *out_refs):
    mine = jnp.concatenate([near_ref[...], far_ref[...]], axis=1)
    total = jnp.dot(own_ref[...], mine, preferred_element_type=f32)
    total += jnp.dot(sibling_ref[...], packed_ref[...], preferred_element_type=f32)
    total = total.astype(bf16)
    for step, out_ref in enumerate(out_refs):

        @pl.when(pl.program_id(0) == step)
        def _(out_ref=out_ref):
            out_ref[...] = total


def project(place, own, sibling, weight, packed, n_y):
    rows, depth = own.shape
    width = weight.shape[1]
    return pl.pallas_call(
        project_kernel,
        out_shape=[jax.ShapeDtypeStruct((rows, 2 * LANES), bf16)] * n_y,
        grid_spec=pltpu.PrefetchScalarGridSpec(
            num_scalar_prefetch=1,
            grid=(n_y,),
            in_specs=[
                pl.BlockSpec((rows, depth), lambda y, _: (0, 0)),
                pl.BlockSpec((rows, depth), lambda y, _: (0, 0)),
                pl.BlockSpec((depth, LANES), lambda y, p: (0, column((y + p[2]) % n_y, p[0], p[1]))),
                pl.BlockSpec((depth, LANES), lambda y, p: (0, column((y + p[2]) % n_y, 1 - p[0], p[1]))),
                pl.BlockSpec((depth, 2 * LANES), lambda y, _: (0, y)),
            ],
            out_specs=[pl.BlockSpec((rows, 2 * LANES), lambda y, _: (0, 0))] * n_y,
        ),
        cost_estimate=pl.CostEstimate(
            flops=2 * rows * depth * width, bytes_accessed=rows * (4 * depth + width) + weight.size * 2, transcendentals=0
        ),
        compiler_params=pltpu.CompilerParams(vmem_limit_bytes=VMEM),
    )(place, own, sibling, weight, weight, packed)


def shift(axis, size, step):
    return [(i, (i + step) % size) for i in range(size)]


def after(array, *earlier):
    return lax.optimization_barrier((array, *earlier))[0]


def exchange(array, axis):
    return lax.all_to_all(array, axis, split_axis=0, concat_axis=0, tiled=True)


def shards(local_weights, base, momentum, tokens, weight):
    sizes = dict(zip(NAMES, SIZES))
    zo, zi, x, y, h, c = (lax.axis_index(a) for a in NAMES)
    n_zo, n_zi, n_x, n_y = (sizes[a] for a in ("zo", "zi", "x", "y"))
    swap = [(0, 1), (1, 0)]
    groups = n_zo * n_zi * n_x
    rows, width = base.shape
    own = rows // groups
    per_x, per_zi = rows // n_x, rows // (n_x * n_zi)

    terms = exchange(local_weights[0].reshape(n_x, per_x, width), "x")

    anchor = lax.dynamic_slice_in_dim(base, x * per_x, per_x, 0).astype(bf16).astype(f32)
    total = terms[0].astype(f32) - n_x * anchor
    for term in range(1, n_x):
        total += terms[term].astype(f32)
    total = total.astype(bf16)

    place = jnp.stack([h, c, y]).astype(jnp.int32)
    sibling = lax.ppermute(tokens, "c", swap)
    packed = lax.ppermute(pack(place, weight, n_y), "c", swap)

    total, sibling, packed = lax.optimization_barrier((total, sibling, packed))
    terms = exchange(total.reshape(n_zi, per_zi, width), "zi")
    part = project(place, tokens, sibling, weight, packed, n_y)
    terms = after(terms, *part)
    total = terms.astype(f32).sum(axis=0).astype(bf16)
    part = [part[0]] + [lax.ppermute(part[step], "y", shift("y", n_y, step)) for step in range(1, n_y)]

    once = 1 + (h >> 4)

    def alone(function, value, shape):
        carry = (value, jnp.zeros(shape, bf16))
        return lax.fori_loop(0, once, lambda _, carry: (-carry[0], function(carry[0])), carry)[1]

    def outer(total):
        across = lax.ppermute(total, "zo", swap)
        outer_grad = (-(total.astype(f32) + across.astype(f32)) / groups).astype(bf16)
        return jnp.broadcast_to(outer_grad, (n_zi, per_zi, width))

    outer_grad = outer(total)
    outer_grad, base, momentum, *part = lax.optimization_barrier((outer_grad, base, momentum, *part))
    gathered = exchange(outer_grad, "zi")

    kv = part[0].astype(f32)
    for piece in range(1, n_y):
        kv += part[piece].astype(f32)
    without = base - 0.567 * momentum
    mine, other, without = lax.optimization_barrier((kv[:, :LANES], kv[:, LANES:].astype(bf16), without))
    gathered, other = lax.optimization_barrier((gathered, other))
    there = lax.ppermute(other, "h", swap)
    gathered = gathered.reshape(per_x, width)
    start = ((zo * n_zi + zi) * n_x + x) * own

    def own_rows(array):
        return lax.dynamic_slice_in_dim(array, start, own, 0).astype(f32)

    def finish(gathered):
        outer_grad = lax.all_gather(gathered, "x", axis=0, tiled=True)
        synced = (without - 1.33 * outer_grad.astype(f32)).astype(bf16)
        new_base = own_rows(without) - 1.33 * own_rows(outer_grad)
        new_momentum = 0.9 * own_rows(momentum) + own_rows(outer_grad)
        return synced, new_base, new_momentum

    empty = (jnp.zeros((rows, width), bf16), jnp.zeros((own, width), f32), jnp.zeros((own, width), f32))
    carry = (gathered, *empty)
    carry = lax.fori_loop(0, once, lambda _, carry: (-carry[0], *finish(carry[0])), carry)
    synced, new_base, new_momentum = carry[1:]
    there = after(there, synced, new_base)
    keys_values = (mine + there.astype(f32)).astype(bf16)
    return new_base, new_momentum, synced, keys_values


def solution(mesh):
    fine = Mesh(mesh.devices.reshape(SIZES), NAMES)
    replica, mp = NAMES[:3], NAMES[3:]
    return jax.shard_map(
        shards,
        mesh=fine,
        in_specs=(
            P(replica, None, mp),
            P(None, mp),
            P(None, mp),
            P(replica, mp),
            P(mp, None),
        ),
        out_specs=(P(replica, mp), P(replica, mp), P(None, mp), P(replica, mp)),
        check_vma=False,
    )
```

```python
import jax
import jax.numpy as jnp
from jax import lax
from jax.experimental import pallas as pl
from jax.experimental.pallas import tpu as pltpu
from jax.sharding import Mesh, PartitionSpec as P

SIZES = (2, 8, 4, 4, 2, 2)
NAMES = ("zo", "zi", "x", "y", "h", "c")
LANES = 128

bf16 = jnp.bfloat16
f32 = jnp.float32
VMEM = 20 << 20


def column(y, h, c):
    return y * 4 + h * 2 + c


def pack_kernel(place_ref, near_ref, far_ref, packed_ref):
    packed_ref[:, :LANES] = near_ref[...]
    packed_ref[:, LANES:] = far_ref[...]


def pack(place, weight, n_y):
    depth, width = weight.shape
    return pl.pallas_call(
        pack_kernel,
        out_shape=jax.ShapeDtypeStruct((depth, width // 2), bf16),
        grid_spec=pltpu.PrefetchScalarGridSpec(
            num_scalar_prefetch=1,
            grid=(n_y,),
            in_specs=[
                pl.BlockSpec((depth, LANES), lambda y, p: (0, column((y + p[2]) % n_y, p[0], 1 - p[1]))),
                pl.BlockSpec((depth, LANES), lambda y, p: (0, column((y + p[2]) % n_y, 1 - p[0], 1 - p[1]))),
            ],
            out_specs=pl.BlockSpec((depth, 2 * LANES), lambda y, _: (0, y)),
        ),
        cost_estimate=pl.CostEstimate(flops=0, bytes_accessed=weight.size * 2, transcendentals=0),
        compiler_params=pltpu.CompilerParams(vmem_limit_bytes=VMEM),
    )(place, weight, weight)


def project_kernel(place_ref, own_ref, sibling_ref, near_ref, far_ref, packed_ref, *out_refs):
    mine = jnp.concatenate([near_ref[...], far_ref[...]], axis=1)
    total = jnp.dot(own_ref[...], mine, preferred_element_type=f32)
    total += jnp.dot(sibling_ref[...], packed_ref[...], preferred_element_type=f32)
    total = total.astype(bf16)
    for step, out_ref in enumerate(out_refs):

        @pl.when(pl.program_id(0) == step)
        def _(out_ref=out_ref):
            out_ref[...] = total


def project(place, own, sibling, weight, packed, n_y):
    rows, depth = own.shape
    width = weight.shape[1]
    return pl.pallas_call(
        project_kernel,
        out_shape=[jax.ShapeDtypeStruct((rows, 2 * LANES), bf16)] * n_y,
        grid_spec=pltpu.PrefetchScalarGridSpec(
            num_scalar_prefetch=1,
            grid=(n_y,),
            in_specs=[
                pl.BlockSpec((rows, depth), lambda y, _: (0, 0)),
                pl.BlockSpec((rows, depth), lambda y, _: (0, 0)),
                pl.BlockSpec((depth, LANES), lambda y, p: (0, column((y + p[2]) % n_y, p[0], p[1]))),
                pl.BlockSpec((depth, LANES), lambda y, p: (0, column((y + p[2]) % n_y, 1 - p[0], p[1]))),
                pl.BlockSpec((depth, 2 * LANES), lambda y, _: (0, y)),
            ],
            out_specs=[pl.BlockSpec((rows, 2 * LANES), lambda y, _: (0, 0))] * n_y,
        ),
        cost_estimate=pl.CostEstimate(
            flops=2 * rows * depth * width, bytes_accessed=rows * (4 * depth + width) + weight.size * 2, transcendentals=0
        ),
        compiler_params=pltpu.CompilerParams(vmem_limit_bytes=VMEM),
    )(place, own, sibling, weight, weight, packed)


def shift(axis, size, step):
    return [(i, (i + step) % size) for i in range(size)]


def after(array, *earlier):
    return lax.optimization_barrier((array, *earlier))[0]


def exchange(array, axis):
    return lax.all_to_all(array, axis, split_axis=0, concat_axis=0, tiled=True)


def shards(local_weights, base, momentum, tokens, weight):
    sizes = dict(zip(NAMES, SIZES))
    zo, zi, x, y, h, c = (lax.axis_index(a) for a in NAMES)
    n_zo, n_zi, n_x, n_y = (sizes[a] for a in ("zo", "zi", "x", "y"))
    swap = [(0, 1), (1, 0)]
    groups = n_zo * n_zi * n_x
    rows, width = base.shape
    own = rows // groups
    per_x, per_zi = rows // n_x, rows // (n_x * n_zi)

    terms = exchange(local_weights[0].reshape(n_x, per_x, width), "x")

    anchor = lax.dynamic_slice_in_dim(base, x * per_x, per_x, 0).astype(bf16).astype(f32)
    total = terms[0].astype(f32) - n_x * anchor
    for term in range(1, n_x):
        total += terms[term].astype(f32)
    total = total.astype(bf16)

    place = jnp.stack([h, c, y]).astype(jnp.int32)
    sibling = lax.ppermute(tokens, "c", swap)
    packed = lax.ppermute(pack(place, weight, n_y), "c", swap)

    total, sibling, packed = lax.optimization_barrier((total, sibling, packed))
    terms = exchange(total.reshape(n_zi, per_zi, width), "zi")
    part = project(place, tokens, sibling, weight, packed, n_y)
    terms = after(terms, *part)
    total = terms.astype(f32).sum(axis=0).astype(bf16)
    part = [part[0]] + [lax.ppermute(part[step], "y", shift("y", n_y, step)) for step in range(1, n_y)]

    once = 1 + (h >> 4)

    def alone(function, value, shape):
        carry = (value, jnp.zeros(shape, bf16))
        return lax.fori_loop(0, once, lambda _, carry: (-carry[0], function(carry[0])), carry)[1]

    def outer(total):
        across = lax.ppermute(total, "zo", swap)
        outer_grad = (-(total.astype(f32) + across.astype(f32)) / groups).astype(bf16)
        return jnp.broadcast_to(outer_grad, (n_zi, per_zi, width))

    outer_grad = outer(total)
    outer_grad, *part = lax.optimization_barrier((outer_grad, *part))
    kv = part[0].astype(f32)
    for piece in range(1, n_y):
        kv += part[piece].astype(f32)
    mine, other = lax.optimization_barrier((kv[:, :LANES], kv[:, LANES:].astype(bf16)))
    there = lax.ppermute(other, "h", swap)
    start = ((zo * n_zi + zi) * n_x + x) * own

    def own_rows(array):
        return lax.dynamic_slice_in_dim(array, start, own, 0).astype(f32)

    def finish(outer_grad):
        outer_grad, old_base, old_momentum = lax.optimization_barrier((outer_grad, base, momentum))
        gathered = exchange(outer_grad, "zi").reshape(per_x, width)
        without = old_base - 0.567 * old_momentum
        gathered, without = lax.optimization_barrier((gathered, without))
        outer_grad = lax.all_gather(gathered, "x", axis=0, tiled=True)
        synced = (without - 1.33 * outer_grad.astype(f32)).astype(bf16)
        new_base = own_rows(without) - 1.33 * own_rows(outer_grad)
        new_momentum = 0.9 * own_rows(old_momentum) + own_rows(outer_grad)
        return synced, new_base, new_momentum

    empty = (jnp.zeros((rows, width), bf16), jnp.zeros((own, width), f32), jnp.zeros((own, width), f32))
    outer_grad = after(outer_grad, other)
    carry = (outer_grad, *empty)
    carry = lax.fori_loop(0, once, lambda _, carry: (-carry[0], *finish(carry[0])), carry)
    synced, new_base, new_momentum = carry[1:]
    there = after(there, synced, new_base)
    keys_values = (mine + there.astype(f32)).astype(bf16)
    return new_base, new_momentum, synced, keys_values


def solution(mesh):
    fine = Mesh(mesh.devices.reshape(SIZES), NAMES)
    replica, mp = NAMES[:3], NAMES[3:]
    return jax.shard_map(
        shards,
        mesh=fine,
        in_specs=(
            P(replica, None, mp),
            P(None, mp),
            P(None, mp),
            P(replica, mp),
            P(mp, None),
        ),
        out_specs=(P(replica, mp), P(replica, mp), P(None, mp), P(replica, mp)),
        check_vma=False,
    )
```

```python
import jax
import jax.numpy as jnp
from jax import lax
from jax.experimental import pallas as pl
from jax.experimental.pallas import tpu as pltpu
from jax.sharding import Mesh, PartitionSpec as P

SIZES = (2, 8, 4, 4, 2, 2)
NAMES = ("zo", "zi", "x", "y", "h", "c")
LANES = 128

bf16 = jnp.bfloat16
f32 = jnp.float32
VMEM = 20 << 20


def column(y, h, c):
    return y * 4 + h * 2 + c


def pack_kernel(place_ref, near_ref, far_ref, packed_ref):
    packed_ref[:, :LANES] = near_ref[...]
    packed_ref[:, LANES:] = far_ref[...]


def pack(place, weight, n_y):
    depth, width = weight.shape
    return pl.pallas_call(
        pack_kernel,
        out_shape=jax.ShapeDtypeStruct((depth, width // 2), bf16),
        grid_spec=pltpu.PrefetchScalarGridSpec(
            num_scalar_prefetch=1,
            grid=(n_y,),
            in_specs=[
                pl.BlockSpec((depth, LANES), lambda y, p: (0, column((y + p[2]) % n_y, p[0], 1 - p[1]))),
                pl.BlockSpec((depth, LANES), lambda y, p: (0, column((y + p[2]) % n_y, 1 - p[0], 1 - p[1]))),
            ],
            out_specs=pl.BlockSpec((depth, 2 * LANES), lambda y, _: (0, y)),
        ),
        cost_estimate=pl.CostEstimate(flops=0, bytes_accessed=weight.size * 2, transcendentals=0),
        compiler_params=pltpu.CompilerParams(vmem_limit_bytes=VMEM),
    )(place, weight, weight)


def project_kernel(place_ref, own_ref, sibling_ref, near_ref, far_ref, packed_ref, *out_refs):
    mine = jnp.concatenate([near_ref[...], far_ref[...]], axis=1)
    lacked = packed_ref[...]
    rows = own_ref.shape[0]
    tile = min(rows, 256)
    for step, out_ref in enumerate(out_refs):

        @pl.when(pl.program_id(0) == step)
        def _(out_ref=out_ref):
            for start in range(0, rows, tile):
                at = slice(start, start + tile)
                total = jnp.dot(own_ref[at, :], mine, preferred_element_type=f32)
                total += jnp.dot(sibling_ref[at, :], lacked, preferred_element_type=f32)
                out_ref[at, :] = total.astype(bf16)


def project(place, own, sibling, weight, packed, n_y):
    rows, depth = own.shape
    width = weight.shape[1]
    return pl.pallas_call(
        project_kernel,
        out_shape=[jax.ShapeDtypeStruct((rows, 2 * LANES), bf16)] * n_y,
        grid_spec=pltpu.PrefetchScalarGridSpec(
            num_scalar_prefetch=1,
            grid=(n_y,),
            in_specs=[
                pl.BlockSpec((rows, depth), lambda y, _: (0, 0)),
                pl.BlockSpec((rows, depth), lambda y, _: (0, 0)),
                pl.BlockSpec((depth, LANES), lambda y, p: (0, column((y + p[2]) % n_y, p[0], p[1]))),
                pl.BlockSpec((depth, LANES), lambda y, p: (0, column((y + p[2]) % n_y, 1 - p[0], p[1]))),
                pl.BlockSpec((depth, 2 * LANES), lambda y, _: (0, y)),
            ],
            out_specs=[pl.BlockSpec((rows, 2 * LANES), lambda y, _: (0, 0))] * n_y,
        ),
        cost_estimate=pl.CostEstimate(
            flops=2 * rows * depth * width, bytes_accessed=rows * (4 * depth + width) + weight.size * 2, transcendentals=0
        ),
        compiler_params=pltpu.CompilerParams(vmem_limit_bytes=VMEM),
    )(place, own, sibling, weight, weight, packed)


def shift(axis, size, step):
    return [(i, (i + step) % size) for i in range(size)]


def after(array, *earlier):
    return lax.optimization_barrier((array, *earlier))[0]


def exchange(array, axis):
    return lax.all_to_all(array, axis, split_axis=0, concat_axis=0, tiled=True)


def shards(local_weights, base, momentum, tokens, weight):
    sizes = dict(zip(NAMES, SIZES))
    zo, zi, x, y, h, c = (lax.axis_index(a) for a in NAMES)
    n_zo, n_zi, n_x, n_y = (sizes[a] for a in ("zo", "zi", "x", "y"))
    swap = [(0, 1), (1, 0)]
    groups = n_zo * n_zi * n_x
    rows, width = base.shape
    own = rows // groups
    per_x, per_zi = rows // n_x, rows // (n_x * n_zi)

    terms = exchange(local_weights[0].reshape(n_x, per_x, width), "x")

    anchor = lax.dynamic_slice_in_dim(base, x * per_x, per_x, 0).astype(bf16).astype(f32)
    total = terms[0].astype(f32) - n_x * anchor
    for term in range(1, n_x):
        total += terms[term].astype(f32)
    total = total.astype(bf16)

    place = jnp.stack([h, c, y]).astype(jnp.int32)
    sibling = lax.ppermute(tokens, "c", swap)
    packed = lax.ppermute(pack(place, weight, n_y), "c", swap)

    total, sibling, packed = lax.optimization_barrier((total, sibling, packed))
    terms = exchange(total.reshape(n_zi, per_zi, width), "zi")
    part = project(place, tokens, sibling, weight, packed, n_y)
    terms = after(terms, *part)
    total = terms.astype(f32).sum(axis=0).astype(bf16)
    part = [part[0]] + [lax.ppermute(part[step], "y", shift("y", n_y, step)) for step in range(1, n_y)]

    once = 1 + (h >> 4)

    def alone(function, value, shape):
        carry = (value, jnp.zeros(shape, bf16))
        return lax.fori_loop(0, once, lambda _, carry: (-carry[0], function(carry[0])), carry)[1]

    def outer(total):
        across = lax.ppermute(total, "zo", swap)
        outer_grad = (-(total.astype(f32) + across.astype(f32)) / groups).astype(bf16)
        return jnp.broadcast_to(outer_grad, (n_zi, per_zi, width))

    outer_grad = outer(total)
    outer_grad, base, momentum, *part = lax.optimization_barrier((outer_grad, base, momentum, *part))
    gathered = exchange(outer_grad, "zi")

    kv = part[0].astype(f32)
    for piece in range(1, n_y):
        kv += part[piece].astype(f32)
    without = base - 0.567 * momentum
    mine, other, without = lax.optimization_barrier((kv[:, :LANES], kv[:, LANES:].astype(bf16), without))
    gathered, other = lax.optimization_barrier((gathered, other))
    there = lax.ppermute(other, "h", swap)
    gathered = gathered.reshape(per_x, width)
    start = ((zo * n_zi + zi) * n_x + x) * own

    def own_rows(array):
        return lax.dynamic_slice_in_dim(array, start, own, 0).astype(f32)

    def finish(gathered):
        outer_grad = lax.all_gather(gathered, "x", axis=0, tiled=True)
        synced = (without - 1.33 * outer_grad.astype(f32)).astype(bf16)
        new_base = own_rows(without) - 1.33 * own_rows(outer_grad)
        new_momentum = 0.9 * own_rows(momentum) + own_rows(outer_grad)
        return synced, new_base, new_momentum

    empty = (jnp.zeros((rows, width), bf16), jnp.zeros((own, width), f32), jnp.zeros((own, width), f32))
    carry = (gathered, *empty)
    carry = lax.fori_loop(0, once, lambda _, carry: (-carry[0], *finish(carry[0])), carry)
    synced, new_base, new_momentum = carry[1:]
    there = after(there, synced, new_base)
    keys_values = (mine + there.astype(f32)).astype(bf16)
    return new_base, new_momentum, synced, keys_values


def solution(mesh):
    fine = Mesh(mesh.devices.reshape(SIZES), NAMES)
    replica, mp = NAMES[:3], NAMES[3:]
    return jax.shard_map(
        shards,
        mesh=fine,
        in_specs=(
            P(replica, None, mp),
            P(None, mp),
            P(None, mp),
            P(replica, mp),
            P(mp, None),
        ),
        out_specs=(P(replica, mp), P(replica, mp), P(None, mp), P(replica, mp)),
        check_vma=False,
    )
```

```python
import jax
import jax.numpy as jnp
from jax import lax
from jax.experimental import pallas as pl
from jax.experimental.pallas import tpu as pltpu
from jax.sharding import Mesh, PartitionSpec as P

SIZES = (2, 8, 4, 4, 2, 2)
NAMES = ("zo", "zi", "x", "y", "h", "c")
LANES = 128

bf16 = jnp.bfloat16
f32 = jnp.float32
VMEM = 20 << 20


def column(y, h, c):
    return y * 4 + h * 2 + c


def pack_kernel(place_ref, near_ref, far_ref, packed_ref):
    packed_ref[:, :LANES] = near_ref[...]
    packed_ref[:, LANES:] = far_ref[...]


def pack(place, weight, n_y):
    depth, width = weight.shape
    return pl.pallas_call(
        pack_kernel,
        out_shape=jax.ShapeDtypeStruct((depth, width // 2), bf16),
        grid_spec=pltpu.PrefetchScalarGridSpec(
            num_scalar_prefetch=1,
            grid=(n_y,),
            in_specs=[
                pl.BlockSpec((depth, LANES), lambda y, p: (0, column((y + p[2]) % n_y, p[0], 1 - p[1]))),
                pl.BlockSpec((depth, LANES), lambda y, p: (0, column((y + p[2]) % n_y, 1 - p[0], 1 - p[1]))),
            ],
            out_specs=pl.BlockSpec((depth, 2 * LANES), lambda y, _: (0, y)),
        ),
        cost_estimate=pl.CostEstimate(flops=0, bytes_accessed=weight.size * 2, transcendentals=0),
        compiler_params=pltpu.CompilerParams(vmem_limit_bytes=VMEM),
    )(place, weight, weight)


def project_kernel(place_ref, own_ref, sibling_ref, near_ref, far_ref, packed_ref, *out_refs):
    mine = jnp.concatenate([near_ref[...], far_ref[...]], axis=1)
    total = jnp.dot(own_ref[...], mine, preferred_element_type=f32)
    total += jnp.dot(sibling_ref[...], packed_ref[...], preferred_element_type=f32)
    total = total.astype(bf16)
    for step, out_ref in enumerate(out_refs):

        @pl.when(pl.program_id(0) == step)
        def _(out_ref=out_ref):
            out_ref[...] = total


def project(place, own, sibling, weight, packed, n_y):
    rows, depth = own.shape
    width = weight.shape[1]
    return pl.pallas_call(
        project_kernel,
        out_shape=[jax.ShapeDtypeStruct((rows, 2 * LANES), bf16)] * n_y,
        grid_spec=pltpu.PrefetchScalarGridSpec(
            num_scalar_prefetch=1,
            grid=(n_y,),
            in_specs=[
                pl.BlockSpec((rows, depth), lambda y, _: (0, 0)),
                pl.BlockSpec((rows, depth), lambda y, _: (0, 0)),
                pl.BlockSpec((depth, LANES), lambda y, p: (0, column((y + p[2]) % n_y, p[0], p[1]))),
                pl.BlockSpec((depth, LANES), lambda y, p: (0, column((y + p[2]) % n_y, 1 - p[0], p[1]))),
                pl.BlockSpec((depth, 2 * LANES), lambda y, _: (0, y)),
            ],
            out_specs=[pl.BlockSpec((rows, 2 * LANES), lambda y, _: (0, 0))] * n_y,
        ),
        cost_estimate=pl.CostEstimate(
            flops=2 * rows * depth * width, bytes_accessed=rows * (4 * depth + width) + weight.size * 2, transcendentals=0
        ),
        compiler_params=pltpu.CompilerParams(vmem_limit_bytes=VMEM),
    )(place, own, sibling, weight, weight, packed)


def shift(axis, size, step):
    return [(i, (i + step) % size) for i in range(size)]


def after(array, *earlier):
    return lax.optimization_barrier((array, *earlier))[0]


def exchange(array, axis):
    return lax.all_to_all(array, axis, split_axis=0, concat_axis=0, tiled=True)


def shards(local_weights, base, momentum, tokens, weight):
    sizes = dict(zip(NAMES, SIZES))
    zo, zi, x, y, h, c = (lax.axis_index(a) for a in NAMES)
    n_zo, n_zi, n_x, n_y = (sizes[a] for a in ("zo", "zi", "x", "y"))
    swap = [(0, 1), (1, 0)]
    groups = n_zo * n_zi * n_x
    rows, width = base.shape
    own = rows // groups
    per_x, per_zi = rows // n_x, rows // (n_x * n_zi)

    terms = exchange(local_weights[0].reshape(n_x, per_x, width), "x")

    anchor = lax.dynamic_slice_in_dim(base, x * per_x, per_x, 0).astype(bf16).astype(f32)
    total = terms[0].astype(f32) - n_x * anchor
    for term in range(1, n_x):
        total += terms[term].astype(f32)
    total = total.astype(bf16)

    place = jnp.stack([h, c, y]).astype(jnp.int32)
    sibling = lax.ppermute(tokens, "c", swap)
    packed = lax.ppermute(pack(place, weight, n_y), "c", swap)

    total, sibling, packed = lax.optimization_barrier((total, sibling, packed))
    terms = exchange(total.reshape(n_zi, per_zi, width), "zi")
    part = project(place, tokens, sibling, weight, packed, n_y)
    terms = after(terms, *part)
    total = terms.astype(f32).sum(axis=0).astype(bf16)
    part = [part[0]] + [lax.ppermute(part[step], "y", shift("y", n_y, step)) for step in range(1, n_y)]

    once = 1 + (h >> 4)

    def alone(function, value, shape):
        carry = (value, jnp.zeros(shape, bf16))
        return lax.fori_loop(0, once, lambda _, carry: (-carry[0], function(carry[0])), carry)[1]

    def outer(total):
        across = lax.ppermute(total, "zo", swap)
        outer_grad = (-(total.astype(f32) + across.astype(f32)) / groups).astype(bf16)
        return jnp.broadcast_to(outer_grad, (n_zi, per_zi, width))

    outer_grad = outer(total)
    outer_grad, base, momentum, *part = lax.optimization_barrier((outer_grad, base, momentum, *part))
    gathered = exchange(outer_grad, "zi")

    kv = part[0].astype(f32)
    for piece in range(1, n_y):
        kv += part[piece].astype(f32)
    without = base - 0.567 * momentum
    mine, other, without = lax.optimization_barrier((kv[:, :LANES], kv[:, LANES:].astype(bf16), without))
    there = lax.ppermute(other, "h", swap)
    gathered = after(gathered, other).reshape(per_x, width)
    start = ((zo * n_zi + zi) * n_x + x) * own

    def own_rows(array):
        return lax.dynamic_slice_in_dim(array, start, own, 0).astype(f32)

    def finish(gathered):
        outer_grad = lax.all_gather(gathered, "x", axis=0, tiled=True)
        synced = (without - 1.33 * outer_grad.astype(f32)).astype(bf16)
        new_base = own_rows(without) - 1.33 * own_rows(outer_grad)
        new_momentum = 0.9 * own_rows(momentum) + own_rows(outer_grad)
        return synced, new_base, new_momentum

    empty = (jnp.zeros((rows, width), bf16), jnp.zeros((own, width), f32), jnp.zeros((own, width), f32))
    carry = (gathered, *empty)
    carry = lax.fori_loop(0, once, lambda _, carry: (-carry[0], *finish(carry[0])), carry)
    synced, new_base, new_momentum = carry[1:]
    there = after(there, synced, new_base)
    keys_values = (mine + there.astype(f32)).astype(bf16)
    return new_base, new_momentum, synced, keys_values


def solution(mesh):
    fine = Mesh(mesh.devices.reshape(SIZES), NAMES)
    replica, mp = NAMES[:3], NAMES[3:]
    return jax.shard_map(
        shards,
        mesh=fine,
        in_specs=(
            P(replica, None, mp),
            P(None, mp),
            P(None, mp),
            P(replica, mp),
            P(mp, None),
        ),
        out_specs=(P(replica, mp), P(replica, mp), P(None, mp), P(replica, mp)),
        check_vma=False,
    )
```
